32 devices in a mesh: section: 4 (over x, core), seq: 8 (over z, y).
Axes of the slice: x: 2, y: 2, z: 4, core: 2. Of those that a mesh axis runs over, the one named last changes fastest.
Arguments:
- hidden: bfloat16 [4, 128, 4096], P('section', 'seq'), may hold values from -6 to 6
- modulation: float32 [4, 3, 4096], P('section'), may hold values from -3 to 3
- w_qkv: bfloat16 [4, 4096, 3, 1024], P('section', None, None, 'seq'), may hold values from -0.09375 to 0.09375
- qk_gain: float32 [4, 2, 128], P('section'), may hold values from 1 to 2.5
- w_out: bfloat16 [4, 1024, 4096], P('section', 'seq'), may hold values from -0.375 to 0.375
- stale_kv: bfloat16 [4, 2, 256, 1024], P('section', None, None, 'seq')
- patch_start: int32 [4], P('section'), may hold values from 0 to 128
Outputs:
- passed: bfloat16 [4, 128, 4096], P('section', 'seq')
The draws below stay inside these ranges and needn't reach their ends.
All inputs are finite; a program needn't handle non-finite values.
Results may differ from the reference program's by a relative error of at most 0.024.
Values may be sent and summed in bfloat16 or wider, within the bound.
No kernel may reach another device: no remote copies, remote signals or barrier semaphores. Data moves between devices by JAX's collectives and lax.ppermute only.
A program may use at most 64 MiB of HBM per device.

```python
import math
import jax
import jax.numpy as jnp
from jax import lax

D = 4096
HD = 128
SECTIONS = 4
HEADS = 8
INNER = 1024
PATCH = 128
CLIP = 256


def draw_stale_kv(key, part):
    base_key = jax.random.fold_in(jax.random.fold_in(key, 7), 0)
    base = jax.random.normal(base_key, (SECTIONS, 2, CLIP, INNER), jnp.float32)
    return base.astype(jnp.bfloat16)


def with_ends(values, key, least, largest):
    spot = [jax.random.randint(jax.random.fold_in(key, axis), (), 0, length) for axis, length in enumerate(values.shape)]
    main_axis = values.shape.index(max(values.shape))
    next_to = spot[:main_axis] + [(spot[main_axis] + 1) % values.shape[main_axis]] + spot[main_axis + 1:]
    return values.at[tuple(spot)].set(least).at[tuple(next_to)].set(largest)


def block_levels(stream_key, shape, shards, smallest, top_value):
    level, own = 1.0, jax.random.fold_in(stream_key, 6)
    for axis_at, shards_of in shards:
        heights = jnp.exp(jax.random.uniform(jax.random.fold_in(own, axis_at), (shards_of,), jnp.float32, smallest / len(shards), top_value / len(shards)))
        level = level * jnp.repeat(heights, shape[axis_at] // shards_of).reshape([-1 if axis == axis_at else 1 for axis in range(len(shape))])
    return level


def noise(stream_key, extent, deviation, bound, cuts=(), held_as=jnp.bfloat16):
    factor_of = block_levels(stream_key, extent, cuts, -0.22, 0.18) if cuts else 1.0
    values = jax.random.normal(stream_key, extent, jnp.float32) * deviation * factor_of
    return jnp.minimum(jnp.maximum(values, -bound), bound).astype(held_as)


def setup_inputs(seed: int = 0) -> dict:
    key_of = jax.random.split(jax.random.key(seed), 8)
    return {
        "hidden": noise(key_of[0], (SECTIONS, PATCH, D), 1.0, 6.0, ((0, 4), (1, 8))),
        "modulation": noise(key_of[1], (SECTIONS, 3, D), 0.6, 3.0, ((0, 4),), jnp.float32),
        "w_qkv": noise(key_of[2], (SECTIONS, D, 3, INNER), D ** -0.5, 0.09375, ((0, 4), (3, 8))),
        "qk_gain": jnp.clip(jnp.exp(math.log(2.5) - 0.916290732 * jax.random.uniform(key_of[3], (SECTIONS, 2, HD), jnp.float32) ** block_levels(key_of[3], (SECTIONS, 2, HD), ((0, 4),), -0.2, 0.2)), 1.0, 2.5),
        "w_out": noise(key_of[4], (SECTIONS, INNER, D), (INNER // 4) ** -0.5, 0.375, ((0, 4), (1, 8))),
        "stale_kv": draw_stale_kv(jax.random.fold_in(key_of[7], 71), 0),
        "patch_start": with_ends(jax.random.randint(key_of[6], (SECTIONS,), 0, CLIP - PATCH + 1), jax.random.fold_in(key_of[6], 1), 0, CLIP - PATCH).astype(jnp.int32),
    }


def modulate(tokens_in, modulation):
    values = tokens_in.astype(jnp.float32)
    average = lax.optimization_barrier(jnp.mean(values, axis=-1, keepdims=True))
    centred = values - average
    spread = lax.optimization_barrier(jnp.mean(centred * centred, axis=-1, keepdims=True))
    normed = centred * lax.rsqrt(spread + 1e-06)
    return (values, (normed * (1.0 + modulation[1]) + modulation[0]).astype(jnp.bfloat16))

def head_norm(values, gains):
    return values * lax.rsqrt(lax.optimization_barrier(jnp.mean(values * values, axis=-1, keepdims=True)) + 1e-06) * gains

def attend(queries, keys_all, values_all):
    scores = jnp.dot(queries, keys_all.T, preferred_element_type=jnp.float32) / math.sqrt(HD)
    highest = lax.optimization_barrier(jnp.max(scores, axis=-1, keepdims=True))
    raised = jnp.exp(scores - highest)
    probs = (raised / lax.optimization_barrier(jnp.sum(raised, axis=-1, keepdims=True))).astype(jnp.bfloat16)
    return jnp.dot(probs, values_all, preferred_element_type=jnp.float32).astype(jnp.bfloat16)

def one_layer(tokens_in, modulation, w_qkv, qk_gain, w_out, stale_kv, patch_start):
    values, mixed = modulate(tokens_in, modulation)
    count = tokens_in.shape[0]
    merged = jnp.dot(mixed, w_qkv.reshape(D, 3 * INNER), preferred_element_type=jnp.float32)
    merged = merged.reshape(count, 3, HEADS, HD)
    queries = head_norm(merged[:, 0], qk_gain[0]).astype(jnp.bfloat16)
    keys_new = head_norm(merged[:, 1], qk_gain[1]).astype(jnp.bfloat16)
    values_new = merged[:, 2].astype(jnp.bfloat16)
    anchor = patch_start.astype(jnp.int32)
    nought = jnp.zeros((), jnp.int32)
    keys_all = lax.dynamic_update_slice(stale_kv[0].reshape(CLIP, HEADS, HD), keys_new, (anchor, nought, nought))
    values_all = lax.dynamic_update_slice(stale_kv[1].reshape(CLIP, HEADS, HD), values_new, (anchor, nought, nought))
    out_heads = w_out.reshape(HEADS, HD, D)

    def per_head(running, items):
        query_h, key_h, value_h, weight_h = items
        attended = attend(query_h, key_h, value_h)
        partial_value = jnp.dot(attended, weight_h, preferred_element_type=jnp.float32).astype(jnp.bfloat16)
        partial_value = lax.optimization_barrier(partial_value)
        return (running + partial_value.astype(jnp.float32), None)
    running, unused = lax.scan(per_head, jnp.zeros((count, D), jnp.float32), (queries.transpose(1, 0, 2), keys_all.transpose(1, 0, 2), values_all.transpose(1, 0, 2), out_heads))
    return (values + modulation[2] * running).astype(jnp.bfloat16)

def reference(hidden, modulation, w_qkv, qk_gain, w_out, stale_kv, patch_start):
    layers = lax.map(lambda items: one_layer(*items), (hidden, modulation, w_qkv, qk_gain, w_out, stale_kv, patch_start))
    return jnp.roll(layers, 1, axis=0)
```

```python
import functools
import math

import jax
import jax.numpy as jnp
from jax import lax
from jax.experimental import pallas as pl
from jax.experimental.pallas import tpu as pltpu
from jax.sharding import PartitionSpec as P


def route(block, distance, sections_on=0):
    sections, count = lax.axis_size("section"), lax.axis_size("seq")
    pairs = [
        (s * count + i, (s + sections_on) % sections * count + (i ^ distance))
        for s in range(sections)
        for i in range(count)
    ]
    return lax.ppermute(block, ("section", "seq"), pairs)


def parents_of(count):
    tree = {r: r & (r - 1) for r in range(1, count)}
    if count == 8:
        tree[7] = 0
    return tree


def gather(block, count):
    tree = parents_of(count)
    blocks = {0: block}
    while len(blocks) < count:
        for r, parent in tree.items():
            if r not in blocks and parent in blocks:
                blocks[r] = route(blocks[parent], r ^ parent)
    return [blocks[r] for r in range(count)]


def layer_kernel(count, start_ref, mod_ref, gain_ref, qkv_ref, stale_ref, out_w_ref, *refs):
    blocks, outs, mixed = refs[:count], refs[count : 2 * count], refs[2 * count]
    rows, width = blocks[0].shape
    head = qkv_ref.shape[2]
    clip = stale_ref.shape[1]
    patch = rows * count
    shift, scale = mod_ref[0:1, :], 1.0 + mod_ref[1:2, :]
    for i, block in enumerate(blocks):
        values = block[...].astype(jnp.float32)
        centred = values - jnp.mean(values, axis=-1, keepdims=True)
        spread = jnp.mean(centred * centred, axis=-1, keepdims=True)
        normed = centred * lax.rsqrt(spread + 1e-06)
        mixed[i * rows : (i + 1) * rows, :] = (normed * scale + shift).astype(jnp.bfloat16)

    def project(j):
        return jnp.dot(mixed[...], qkv_ref[j], preferred_element_type=jnp.float32)

    def head_norm(values, gains):
        return values * lax.rsqrt(jnp.mean(values * values, axis=-1, keepdims=True) + 1e-06) * gains

    queries = head_norm(project(0), gain_ref[0:1, :]).astype(jnp.bfloat16)
    keys_new = head_norm(project(1), gain_ref[1:2, :]).astype(jnp.bfloat16)
    values_new = project(2).astype(jnp.bfloat16)

    def scores_of(keys):
        raw = lax.dot_general(queries, keys, (((1,), (1,)), ((), ())), preferred_element_type=jnp.float32)
        return raw * (1.0 / math.sqrt(head))

    start = start_ref[0]
    clip_row = lax.broadcasted_iota(jnp.int32, (patch, clip), 1)
    replaced = (clip_row >= start) & (clip_row < start + patch)
    scores_new = scores_of(keys_new)
    scores_old = jnp.where(replaced, -jnp.inf, scores_of(stale_ref[0]))
    highest = jnp.maximum(
        jnp.max(scores_new, axis=-1, keepdims=True), jnp.max(scores_old, axis=-1, keepdims=True)
    )
    raised_new = jnp.exp(scores_new - highest)
    raised_old = jnp.exp(scores_old - highest)
    summed = jnp.sum(raised_new, axis=-1, keepdims=True) + jnp.sum(raised_old, axis=-1, keepdims=True)
    probs_new = (raised_new / summed).astype(jnp.bfloat16)
    probs_old = (raised_old / summed).astype(jnp.bfloat16)
    attended = jnp.dot(probs_new, values_new, preferred_element_type=jnp.float32) + jnp.dot(
        probs_old, stale_ref[1], preferred_element_type=jnp.float32
    )
    attended = attended.astype(jnp.bfloat16)
    step = 512
    for at in range(0, width, step):
        columns = slice(at, at + step)
        part = jnp.dot(attended, out_w_ref[:, columns], preferred_element_type=jnp.float32)
        part = part * mod_ref[2:3, columns]
        for r, out in enumerate(outs):
            piece = part[r * rows : (r + 1) * rows]
            if r == 0:
                piece = piece + blocks[0][:, columns].astype(jnp.float32)
            out[:, columns] = piece.astype(jnp.bfloat16)


def add_up(*blocks):
    total = blocks[0].astype(jnp.float32)
    for block in blocks[1:]:
        total = total + block.astype(jnp.float32)
    return total.astype(jnp.bfloat16)


def reduce_scatter(parts, count):
    tree = parents_of(count)
    arrived = {r: [] for r in range(count)}
    waiting = set(tree)
    while waiting:
        ready = [r for r in waiting if not any(tree[c] == r for c in waiting)]
        moved = [(r, route(add_up(parts[r], *arrived[r]), r ^ tree[r], int(tree[r] == 0))) for r in ready]
        for r, block in moved:
            arrived[tree[r]].append(block)
            waiting.discard(r)
    own = route(parts[0], 0, 1)
    return add_up(own, *arrived[0])


def per_device(hidden, modulation, w_qkv, qk_gain, w_out, stale_kv, patch_start):
    count = lax.axis_size("seq")
    tokens_in = hidden[0]
    rows, width = tokens_in.shape
    blocks = gather(tokens_in, count)
    vmem = pl.BlockSpec(memory_space=pltpu.VMEM)
    parts = pl.pallas_call(
        functools.partial(layer_kernel, count),
        out_shape=[jax.ShapeDtypeStruct((rows, width), jnp.bfloat16)] * count,
        in_specs=[pl.BlockSpec(memory_space=pltpu.SMEM)] + [vmem] * (5 + count),
        out_specs=[vmem] * count,
        scratch_shapes=[pltpu.VMEM((rows * count, width), jnp.bfloat16)],
        compiler_params=pltpu.CompilerParams(vmem_limit_bytes=40 * 2**20),
        name="layer",
    )(
        patch_start,
        modulation[0],
        qk_gain[0],
        w_qkv[0].transpose(1, 0, 2),
        stale_kv[0],
        w_out[0],
        *blocks,
    )
    return reduce_scatter(parts, count)[None]


def solution(mesh):
    in_specs = (
        P("section", "seq", None),
        P("section", None, None),
        P("section", None, None, "seq"),
        P("section", None, None),
        P("section", "seq", None),
        P("section", None, None, "seq"),
        P("section"),
    )
    out_specs = P("section", "seq", None)
    return jax.shard_map(
        per_device, mesh=mesh, in_specs=in_specs, out_specs=out_specs, check_vma=False
    )
```

```python
import functools
import math

import jax
import jax.numpy as jnp
from jax import lax
from jax.experimental import pallas as pl
from jax.experimental.pallas import tpu as pltpu
from jax.sharding import PartitionSpec as P


def route(block, distance, sections_on=0):
    sections, count = lax.axis_size("section"), lax.axis_size("seq")
    pairs = [
        (s * count + i, (s + sections_on) % sections * count + (i ^ distance))
        for s in range(sections)
        for i in range(count)
    ]
    return lax.ppermute(block, ("section", "seq"), pairs)


def plan(count):
    if count == 8:
        return [(1, 0), (2, 0), (3, 2), (4, 0), (5, 4), (6, 4), (7, 1)]
    return [(r, r & (r - 1)) for r in range(1, count)]


def plan_back(count):
    if count == 8:
        return [(5, 4), (6, 4), (4, 0), (3, 2), (2, 0), (7, 1), (1, 0), (0, 0)]
    return [(r, r & (r - 1)) for r in reversed(range(count))]


def gather(block, count):
    blocks = {0: block}
    for r, parent in plan(count):
        blocks[r] = route(blocks[parent], r ^ parent)
    return blocks


def modulated(block, mod_ref):
    values = block.astype(jnp.float32)
    centred = values - jnp.mean(values, axis=-1, keepdims=True)
    spread = jnp.mean(centred * centred, axis=-1, keepdims=True)
    normed = centred * lax.rsqrt(spread + 1e-06)
    return (normed * (1.0 + mod_ref[1]) + mod_ref[0]).astype(jnp.bfloat16)


def early_kernel(mod_ref, *refs):
    blocks, mixed_ref = refs[:-1], refs[-1]
    rows = blocks[0].shape[0]
    for i, block in enumerate(blocks):
        mixed_ref[i * rows : (i + 1) * rows, :] = modulated(block[...], mod_ref)


def early_rows(mod, blocks):
    rows, width = blocks[0].shape
    vmem = pl.BlockSpec(memory_space=pltpu.VMEM)
    return pl.pallas_call(
        early_kernel,
        out_shape=jax.ShapeDtypeStruct((rows * len(blocks), width), jnp.bfloat16),
        in_specs=[vmem] * (1 + len(blocks)),
        out_specs=vmem,
        compiler_params=pltpu.CompilerParams(vmem_limit_bytes=12 * 2**20),
        cost_estimate=pl.CostEstimate(flops=2 * 10**9, bytes_accessed=blocks[0].size * 64, transcendentals=0),
        name="early",
    )(mod, *blocks)


def layer_kernel(count, start_ref, mod_ref, qkv_ref, stale_ref, out_w_ref, gain_ref, mixed_ref, own_ref, *refs):
    late = len(refs) - 1 - count
    blocks, outs, mixed = refs[:late], refs[late : late + count], refs[late + count]
    rows, width = own_ref.shape
    head = qkv_ref.shape[2]
    clip = stale_ref.shape[1]
    patch = rows * count
    first = mixed_ref.shape[0]
    mixed[:first, :] = mixed_ref[...]
    for i, block in enumerate(blocks):
        mixed[first + i * rows : first + (i + 1) * rows, :] = modulated(block[...], mod_ref)

    def project(j):
        return jnp.dot(mixed[...], qkv_ref[j], preferred_element_type=jnp.float32)

    def head_norm(values, gains):
        return values * lax.rsqrt(jnp.mean(values * values, axis=-1, keepdims=True) + 1e-06) * gains

    queries = head_norm(project(0), gain_ref[0:1, :]).astype(jnp.bfloat16)
    keys_new = head_norm(project(1), gain_ref[1:2, :]).astype(jnp.bfloat16)
    values_new = project(2).astype(jnp.bfloat16)

    def scores_of(keys):
        raw = lax.dot_general(queries, keys, (((1,), (1,)), ((), ())), preferred_element_type=jnp.float32)
        return raw * (1.0 / math.sqrt(head))

    start = start_ref[0]
    clip_row = lax.broadcasted_iota(jnp.int32, (patch, clip), 1)
    replaced = (clip_row >= start) & (clip_row < start + patch)
    scores_new = scores_of(keys_new)
    scores_old = jnp.where(replaced, -jnp.inf, scores_of(stale_ref[0]))
    highest = jnp.maximum(
        jnp.max(scores_new, axis=-1, keepdims=True), jnp.max(scores_old, axis=-1, keepdims=True)
    )
    raised_new = jnp.exp(scores_new - highest)
    raised_old = jnp.exp(scores_old - highest)
    summed = jnp.sum(raised_new, axis=-1, keepdims=True) + jnp.sum(raised_old, axis=-1, keepdims=True)
    probs_new = (raised_new / summed).astype(jnp.bfloat16)
    probs_old = (raised_old / summed).astype(jnp.bfloat16)
    attended = jnp.dot(probs_new, values_new, preferred_element_type=jnp.float32) + jnp.dot(
        probs_old, stale_ref[1], preferred_element_type=jnp.float32
    )
    attended = attended.astype(jnp.bfloat16)
    step = 512
    for at in range(0, width, step):
        columns = slice(at, at + step)
        part = jnp.dot(attended, out_w_ref[:, columns], preferred_element_type=jnp.float32)
        part = part * mod_ref[2, :, columns]
        for r, out in enumerate(outs):
            piece = part[r * rows : (r + 1) * rows]
            if r == 0:
                piece = piece + own_ref[:, columns].astype(jnp.float32)
            out[:, columns] = piece.astype(jnp.bfloat16)


def add_up(*blocks):
    total = blocks[0].astype(jnp.float32)
    for block in blocks[1:]:
        total = total + block.astype(jnp.float32)
    return total.astype(jnp.bfloat16)


def reduce_scatter(parts, count):
    arrived = {r: [] for r in range(count)}
    for r, target in plan_back(count):
        if r == 0:
            arrived[0].append(route(parts[0], 0, 1))
        else:
            arrived[target].append(route(add_up(parts[r], *arrived[r]), r ^ target, int(target == 0)))
    return add_up(*arrived[0])


def per_device(hidden, modulation, w_qkv, qk_gain, w_out, stale_kv, patch_start):
    count = lax.axis_size("seq")
    tokens_in = hidden[0]
    rows, width = tokens_in.shape
    blocks = gather(tokens_in, count)
    order = [0, 2, 1, 3, 4, 5, 6, 7] if count == 8 else list(range(count))
    mod, own = modulation.transpose(1, 0, 2), tokens_in
    early = 2
    mixed = early_rows(mod, [blocks[r] for r in order[:early]])
    vmem = pl.BlockSpec(memory_space=pltpu.VMEM)
    late = [blocks[r] for r in order[early:]]
    parts = pl.pallas_call(
        functools.partial(layer_kernel, count),
        out_shape=[jax.ShapeDtypeStruct((rows, width), jnp.bfloat16)] * count,
        in_specs=[pl.BlockSpec(memory_space=pltpu.SMEM)] + [vmem] * (7 + len(late)),
        out_specs=[vmem] * count,
        scratch_shapes=[pltpu.VMEM((rows * count, width), jnp.bfloat16)],
        compiler_params=pltpu.CompilerParams(vmem_limit_bytes=(12 + count) * 2**20),
        name="layer",
    )(patch_start, mod, w_qkv[0].transpose(1, 0, 2), stale_kv[0], w_out[0], qk_gain[0], mixed, own, *late)
    return reduce_scatter(dict(zip(order, parts)), count)[None]


def solution(mesh):
    in_specs = (
        P("section", "seq", None),
        P("section", None, None),
        P("section", None, None, "seq"),
        P("section", None, None),
        P("section", "seq", None),
        P("section", None, None, "seq"),
        P("section"),
    )
    out_specs = P("section", "seq", None)
    return jax.shard_map(
        per_device, mesh=mesh, in_specs=in_specs, out_specs=out_specs, check_vma=False
    )
```

```python
import functools
import math

import jax
import jax.numpy as jnp
from jax import lax
from jax.experimental import pallas as pl
from jax.experimental.pallas import tpu as pltpu
from jax.sharding import PartitionSpec as P


def route(block, distance, sections_on=0):
    sections, count = lax.axis_size("section"), lax.axis_size("seq")
    pairs = [
        (s * count + i, (s + sections_on) % sections * count + (i ^ distance))
        for s in range(sections)
        for i in range(count)
    ]
    return lax.ppermute(block, ("section", "seq"), pairs)


def plan(count):
    if count == 8:
        return [(1, 0), (2, 0), (3, 0), (4, 0), (5, 4), (6, 4), (7, 1)]
    return [(r, r & (r - 1)) for r in range(1, count)]


def plan_back(count):
    if count == 8:
        return [(5, 4), (6, 4), (4, 0), (3, 2), (2, 0), (7, 1), (1, 0), (0, 0)]
    return [(r, r & (r - 1)) for r in reversed(range(count))]


def after(block, other):
    return lax.optimization_barrier((block, other))[0]


def gather(block, count, mixed):
    blocks = {0: block}
    for r, parent in plan(count):
        blocks[r] = route(blocks[parent], r ^ parent)
        if r == 4:
            blocks[r] = after(blocks[r], mixed)
    return blocks


def modulated(block, mod_ref):
    values = block.astype(jnp.float32)
    centred = values - jnp.mean(values, axis=-1, keepdims=True)
    spread = jnp.mean(centred * centred, axis=-1, keepdims=True)
    normed = centred * lax.rsqrt(spread + 1e-06)
    return (normed * (1.0 + mod_ref[1]) + mod_ref[0]).astype(jnp.bfloat16)


def early_kernel(mod_ref, *refs):
    blocks, mixed_ref = refs[:-1], refs[-1]
    rows = blocks[0].shape[0]
    for i, block in enumerate(blocks):
        mixed_ref[i * rows : (i + 1) * rows, :] = modulated(block[...], mod_ref)


def early_rows(mod, blocks):
    rows, width = blocks[0].shape
    vmem = pl.BlockSpec(memory_space=pltpu.VMEM)
    return pl.pallas_call(
        early_kernel,
        out_shape=jax.ShapeDtypeStruct((rows * len(blocks), width), jnp.bfloat16),
        in_specs=[vmem] * (1 + len(blocks)),
        out_specs=vmem,
        compiler_params=pltpu.CompilerParams(vmem_limit_bytes=12 * 2**20),
        cost_estimate=pl.CostEstimate(flops=2 * 10**9, bytes_accessed=64 * blocks[0].size, transcendentals=0),
        name="early",
    )(mod, *blocks)


def heads_of(mixed, gain_ref, qkv_ref):
    def part(j):
        return jnp.dot(mixed, qkv_ref[j], preferred_element_type=jnp.float32)

    def head_norm(values, gains):
        return values * lax.rsqrt(jnp.mean(values * values, axis=-1, keepdims=True) + 1e-06) * gains

    queries = head_norm(part(0), gain_ref[0:1, :]).astype(jnp.bfloat16)
    keys = head_norm(part(1), gain_ref[1:2, :]).astype(jnp.bfloat16)
    return queries, keys, part(2).astype(jnp.bfloat16)


def modulate_into(mixed, at, blocks, mod_ref):
    for block in blocks:
        mixed[at : at + block.shape[0], :] = modulated(block[...], mod_ref)
        at += block.shape[0]


def middle_kernel(mod_ref, gain_ref, qkv_ref, mixed_ref, *refs):
    blocks, heads_ref, mixed = refs[:-2], refs[-2], refs[-1]
    first = mixed_ref.shape[0]
    mixed[:first, :] = mixed_ref[...]
    modulate_into(mixed, first, blocks, mod_ref)
    for j, part in enumerate(heads_of(mixed[...], gain_ref, qkv_ref)):
        heads_ref[j] = part


def middle_heads(mod, gains, qkv, mixed, blocks):
    vmem = pl.BlockSpec(memory_space=pltpu.VMEM)
    tokens = mixed.shape[0] + sum(block.shape[0] for block in blocks)
    width, head = qkv.shape[1:]
    return pl.pallas_call(
        middle_kernel,
        out_shape=jax.ShapeDtypeStruct((3, tokens, head), jnp.bfloat16),
        in_specs=[vmem] * (4 + len(blocks)),
        out_specs=vmem,
        scratch_shapes=[pltpu.VMEM((tokens, width), jnp.bfloat16)],
        compiler_params=pltpu.CompilerParams(vmem_limit_bytes=24 * 2**20),
        cost_estimate=pl.CostEstimate(flops=10**9, bytes_accessed=2 * qkv.size, transcendentals=0),
        name="middle",
    )(mod, gains, qkv, mixed, *blocks)


def layer_kernel(count, outs_of, start_ref, mod_ref, qkv_ref, stale_ref, out_w_ref, gain_ref, heads_ref, own_ref, *refs):
    rows, width = own_ref.shape
    number = len(outs_of) + 1
    blocks, outs, attended_ref, mixed = refs[: -1 - number], refs[-1 - number : -2], refs[-2], refs[-1]
    head = qkv_ref.shape[2]
    clip = stale_ref.shape[1]
    patch = rows * count
    modulate_into(mixed, 0, blocks, mod_ref)
    queries, keys_new, values_new = [
        jnp.concatenate([heads_ref[j], part], axis=0)
        for j, part in enumerate(heads_of(mixed[...], gain_ref, qkv_ref))
    ]

    def scores_of(keys):
        raw = lax.dot_general(queries, keys, (((1,), (1,)), ((), ())), preferred_element_type=jnp.float32)
        return raw * (1.0 / math.sqrt(head))

    start = start_ref[0]
    clip_row = lax.broadcasted_iota(jnp.int32, (patch, clip), 1)
    replaced = (clip_row >= start) & (clip_row < start + patch)
    scores_new = scores_of(keys_new)
    scores_old = jnp.where(replaced, -jnp.inf, scores_of(stale_ref[0]))
    highest = jnp.maximum(
        jnp.max(scores_new, axis=-1, keepdims=True), jnp.max(scores_old, axis=-1, keepdims=True)
    )
    raised_new = jnp.exp(scores_new - highest)
    raised_old = jnp.exp(scores_old - highest)
    summed = jnp.sum(raised_new, axis=-1, keepdims=True) + jnp.sum(raised_old, axis=-1, keepdims=True)
    probs_new = (raised_new / summed).astype(jnp.bfloat16)
    probs_old = (raised_old / summed).astype(jnp.bfloat16)
    attended = jnp.dot(probs_new, values_new, preferred_element_type=jnp.float32) + jnp.dot(
        probs_old, stale_ref[1], preferred_element_type=jnp.float32
    )
    attended = attended.astype(jnp.bfloat16)
    attended_ref[...] = attended
    project_out(attended, outs_of, outs, mod_ref, out_w_ref, own_ref)


def project_out(attended, outs_of, outs, mod_ref, out_w_ref, own_ref):
    rows, width = own_ref.shape
    chosen = jnp.concatenate([attended[i * rows : (i + 1) * rows] for i in outs_of], axis=0)
    step = 512
    for at in range(0, width, step):
        columns = slice(at, at + step)
        part = jnp.dot(chosen, out_w_ref[:, columns], preferred_element_type=jnp.float32)
        part = part * mod_ref[2, :, columns]
        for k, out in enumerate(outs):
            piece = part[k * rows : (k + 1) * rows]
            if outs_of[k] == 0:
                piece = piece + own_ref[:, columns].astype(jnp.float32)
            out[:, columns] = piece.astype(jnp.bfloat16)


def rest_kernel(outs_of, mod_ref, out_w_ref, own_ref, attended_ref, *outs):
    project_out(attended_ref[...], outs_of, outs, mod_ref, out_w_ref, own_ref)


def add_up(*blocks):
    total = blocks[0].astype(jnp.float32)
    for block in blocks[1:]:
        total = total + block.astype(jnp.float32)
    return total.astype(jnp.bfloat16)


def reduce_scatter(parts, count):
    arrived = {r: [] for r in range(count)}
    for r, target in plan_back(count):
        total = add_up(parts[r], *arrived[r]) if r and arrived[r] else parts[r]
        arrived[target].append(route(total, r ^ target, int(target == 0)))
    return add_up(*arrived[0])


def per_device(hidden, modulation, w_qkv, qk_gain, w_out, stale_kv, patch_start):
    count = lax.axis_size("seq")
    tokens_in = hidden[0]
    rows, width = tokens_in.shape
    order = [0, 1, 2, 3, 7, 4, 5, 6] if count == 8 else list(range(count))
    mod, own = modulation.transpose(1, 0, 2), tokens_in
    mixed = early_rows(mod, [own])
    blocks = gather(tokens_in, count, mixed)
    vmem = pl.BlockSpec(memory_space=pltpu.VMEM)
    middle = count - 2
    qkv, gains = w_qkv[0].transpose(1, 0, 2), qk_gain[0]
    heads = middle_heads(mod, gains, qkv, mixed, [blocks[r] for r in order[1:middle]])
    late = [blocks[r] for r in order[middle:]]
    first = [order.index(r) for r in (count - 3, count - 2)]
    rest = [i for i in range(count) if i not in first]
    shape = jax.ShapeDtypeStruct((rows, width), jnp.bfloat16)
    head = qkv.shape[2]
    *parts, attended = pl.pallas_call(
        functools.partial(layer_kernel, count, first),
        out_shape=[shape] * len(first) + [jax.ShapeDtypeStruct((rows * count, head), jnp.bfloat16)],
        in_specs=[pl.BlockSpec(memory_space=pltpu.SMEM)] + [vmem] * (7 + len(late)),
        out_specs=[vmem] * (len(first) + 1),
        scratch_shapes=[pltpu.VMEM((rows * (count - middle), width), jnp.bfloat16)],
        compiler_params=pltpu.CompilerParams(vmem_limit_bytes=24 * 2**20),
        name="layer",
    )(patch_start, mod, qkv, stale_kv[0], w_out[0], gains, heads, own, *late)
    if rest:
        parts += pl.pallas_call(
            functools.partial(rest_kernel, rest),
            out_shape=[shape] * len(rest),
            in_specs=[vmem] * 4,
            out_specs=[vmem] * len(rest),
            compiler_params=pltpu.CompilerParams(vmem_limit_bytes=24 * 2**20),
            name="rest",
        )(mod, w_out[0], own, attended)
    parts = {order[i]: part for i, part in zip(first + rest, parts)}
    return reduce_scatter(parts, count)[None]


def solution(mesh):
    in_specs = (
        P("section", "seq", None),
        P("section", None, None),
        P("section", None, None, "seq"),
        P("section", None, None),
        P("section", "seq", None),
        P("section", None, None, "seq"),
        P("section"),
    )
    out_specs = P("section", "seq", None)
    return jax.shard_map(
        per_device, mesh=mesh, in_specs=in_specs, out_specs=out_specs, check_vma=False
    )
```

```python
import functools
import math

import jax
import jax.numpy as jnp
from jax import lax
from jax.experimental import pallas as pl
from jax.experimental.pallas import tpu as pltpu
from jax.sharding import PartitionSpec as P


def route(block, distance, sections_on=0):
    sections, count = lax.axis_size("section"), lax.axis_size("seq")
    pairs = [
        (s * count + i, (s + sections_on) % sections * count + (i ^ distance))
        for s in range(sections)
        for i in range(count)
    ]
    return lax.ppermute(block, ("section", "seq"), pairs)


def plan(count):
    if count == 8:
        return [(1, 0), (2, 0), (3, 0), (4, 0), (5, 4), (6, 4), (7, 4)]
    return [(r, r & (r - 1)) for r in range(1, count)]


def plan_back(count):
    if count == 8:
        return [(5, 4), (6, 4), (4, 0), (3, 2), (2, 0), (7, 1), (1, 0), (0, 0)]
    return [(r, r & (r - 1)) for r in reversed(range(count))]


def after(block, other):
    return lax.optimization_barrier((block, other))[0]


def gather(block, count, mixed):
    blocks = {0: block}
    for r, parent in plan(count):
        blocks[r] = route(blocks[parent], r ^ parent)
        if r == 4:
            blocks[r] = after(blocks[r], mixed)
    return blocks


def modulated(block, mod_ref):
    values = block.astype(jnp.float32)
    centred = values - jnp.mean(values, axis=-1, keepdims=True)
    spread = jnp.mean(centred * centred, axis=-1, keepdims=True)
    normed = centred * lax.rsqrt(spread + 1e-06)
    return (normed * (1.0 + mod_ref[1]) + mod_ref[0]).astype(jnp.bfloat16)


def early_kernel(mod_ref, *refs):
    blocks, mixed_ref = refs[:-1], refs[-1]
    rows = blocks[0].shape[0]
    for i, block in enumerate(blocks):
        mixed_ref[i * rows : (i + 1) * rows, :] = modulated(block[...], mod_ref)


def early_rows(mod, blocks):
    rows, width = blocks[0].shape
    vmem = pl.BlockSpec(memory_space=pltpu.VMEM)
    return pl.pallas_call(
        early_kernel,
        out_shape=jax.ShapeDtypeStruct((rows * len(blocks), width), jnp.bfloat16),
        in_specs=[vmem] * (1 + len(blocks)),
        out_specs=vmem,
        compiler_params=pltpu.CompilerParams(vmem_limit_bytes=12 * 2**20),
        cost_estimate=pl.CostEstimate(flops=2 * 10**9, bytes_accessed=64 * blocks[0].size, transcendentals=0),
        name="early",
    )(mod, *blocks)


def heads_of(mixed, gain_ref, qkv_ref):
    def part(j):
        return jnp.dot(mixed, qkv_ref[j], preferred_element_type=jnp.float32)

    def head_norm(values, gains):
        return values * lax.rsqrt(jnp.mean(values * values, axis=-1, keepdims=True) + 1e-06) * gains

    queries = head_norm(part(0), gain_ref[0:1, :]).astype(jnp.bfloat16)
    keys = head_norm(part(1), gain_ref[1:2, :]).astype(jnp.bfloat16)
    return queries, keys, part(2).astype(jnp.bfloat16)


def modulate_into(mixed, at, blocks, mod_ref):
    for block in blocks:
        mixed[at : at + block.shape[0], :] = modulated(block[...], mod_ref)
        at += block.shape[0]


def middle_kernel(mod_ref, gain_ref, qkv_ref, mixed_ref, *refs):
    blocks, heads_ref, mixed = refs[:-2], refs[-2], refs[-1]
    first = mixed_ref.shape[0]
    mixed[:first, :] = mixed_ref[...]
    modulate_into(mixed, first, blocks, mod_ref)
    for j, part in enumerate(heads_of(mixed[...], gain_ref, qkv_ref)):
        heads_ref[j] = part


def middle_heads(mod, gains, qkv, mixed, blocks):
    vmem = pl.BlockSpec(memory_space=pltpu.VMEM)
    tokens = mixed.shape[0] + sum(block.shape[0] for block in blocks)
    width, head = qkv.shape[1:]
    return pl.pallas_call(
        middle_kernel,
        out_shape=jax.ShapeDtypeStruct((3, tokens, head), jnp.bfloat16),
        in_specs=[vmem] * (4 + len(blocks)),
        out_specs=vmem,
        scratch_shapes=[pltpu.VMEM((tokens, width), jnp.bfloat16)],
        compiler_params=pltpu.CompilerParams(vmem_limit_bytes=24 * 2**20),
        cost_estimate=pl.CostEstimate(flops=10**9, bytes_accessed=2 * qkv.size, transcendentals=0),
        name="middle",
    )(mod, gains, qkv, mixed, *blocks)


def layer_kernel(count, outs_of, start_ref, mod_ref, qkv_ref, stale_ref, out_w_ref, gain_ref, heads_ref, own_ref, *refs):
    rows, width = own_ref.shape
    number = len(outs_of) + 1
    blocks, outs, attended_ref, mixed = refs[: -1 - number], refs[-1 - number : -2], refs[-2], refs[-1]
    head = qkv_ref.shape[2]
    clip = stale_ref.shape[1]
    patch = rows * count
    modulate_into(mixed, 0, blocks, mod_ref)
    queries, keys_new, values_new = [
        jnp.concatenate([heads_ref[j], part], axis=0)
        for j, part in enumerate(heads_of(mixed[...], gain_ref, qkv_ref))
    ]

    def scores_of(keys):
        raw = lax.dot_general(queries, keys, (((1,), (1,)), ((), ())), preferred_element_type=jnp.float32)
        return raw * (1.0 / math.sqrt(head))

    start = start_ref[0]
    clip_row = lax.broadcasted_iota(jnp.int32, (patch, clip), 1)
    replaced = (clip_row >= start) & (clip_row < start + patch)
    scores_new = scores_of(keys_new)
    scores_old = jnp.where(replaced, -jnp.inf, scores_of(stale_ref[0]))
    highest = jnp.maximum(
        jnp.max(scores_new, axis=-1, keepdims=True), jnp.max(scores_old, axis=-1, keepdims=True)
    )
    raised_new = jnp.exp(scores_new - highest)
    raised_old = jnp.exp(scores_old - highest)
    summed = jnp.sum(raised_new, axis=-1, keepdims=True) + jnp.sum(raised_old, axis=-1, keepdims=True)
    probs_new = (raised_new / summed).astype(jnp.bfloat16)
    probs_old = (raised_old / summed).astype(jnp.bfloat16)
    attended = jnp.dot(probs_new, values_new, preferred_element_type=jnp.float32) + jnp.dot(
        probs_old, stale_ref[1], preferred_element_type=jnp.float32
    )
    attended = attended.astype(jnp.bfloat16)
    attended_ref[...] = attended
    project_out(attended, outs_of, outs, mod_ref, out_w_ref, own_ref)


def project_out(attended, outs_of, outs, mod_ref, out_w_ref, own_ref):
    rows, width = own_ref.shape
    chosen = jnp.concatenate([attended[i * rows : (i + 1) * rows] for i in outs_of], axis=0)
    step = 512
    for at in range(0, width, step):
        columns = slice(at, at + step)
        part = jnp.dot(chosen, out_w_ref[:, columns], preferred_element_type=jnp.float32)
        part = part * mod_ref[2, :, columns]
        for k, out in enumerate(outs):
            piece = part[k * rows : (k + 1) * rows]
            if outs_of[k] == 0:
                piece = piece + own_ref[:, columns].astype(jnp.float32)
            out[:, columns] = piece.astype(jnp.bfloat16)


def rest_kernel(outs_of, mod_ref, out_w_ref, own_ref, attended_ref, *outs):
    project_out(attended_ref[...], outs_of, outs, mod_ref, out_w_ref, own_ref)


def add_up(*blocks):
    total = blocks[0].astype(jnp.float32)
    for block in blocks[1:]:
        total = total + block.astype(jnp.float32)
    return total.astype(jnp.bfloat16)


def reduce_scatter(parts, count):
    arrived = {r: [] for r in range(count)}
    for r, target in plan_back(count):
        total = add_up(parts[r], *arrived[r]) if r and arrived[r] else parts[r]
        arrived[target].append(route(total, r ^ target, int(target == 0)))
    return add_up(*arrived[0])


def per_device(hidden, modulation, w_qkv, qk_gain, w_out, stale_kv, patch_start):
    count = lax.axis_size("seq")
    tokens_in = hidden[0]
    rows, width = tokens_in.shape
    order = [0, 1, 2, 3, 4, 7, 6, 5] if count == 8 else list(range(count))
    mod, own = modulation.transpose(1, 0, 2), tokens_in
    mixed = early_rows(mod, [own])
    blocks = gather(tokens_in, count, mixed)
    vmem = pl.BlockSpec(memory_space=pltpu.VMEM)
    middle = count - 2
    qkv, gains = w_qkv[0].transpose(1, 0, 2), qk_gain[0]
    heads = middle_heads(mod, gains, qkv, mixed, [blocks[r] for r in order[1:middle]])
    late = [blocks[r] for r in order[middle:]]
    first = [order.index(r) for r in (count - 3, count - 2)]
    rest = [i for i in range(count) if i not in first]
    shape = jax.ShapeDtypeStruct((rows, width), jnp.bfloat16)
    head = qkv.shape[2]
    *parts, attended = pl.pallas_call(
        functools.partial(layer_kernel, count, first),
        out_shape=[shape] * len(first) + [jax.ShapeDtypeStruct((rows * count, head), jnp.bfloat16)],
        in_specs=[pl.BlockSpec(memory_space=pltpu.SMEM)] + [vmem] * (7 + len(late)),
        out_specs=[vmem] * (len(first) + 1),
        scratch_shapes=[pltpu.VMEM((rows * (count - middle), width), jnp.bfloat16)],
        compiler_params=pltpu.CompilerParams(vmem_limit_bytes=24 * 2**20),
        name="layer",
    )(patch_start, mod, qkv, stale_kv[0], w_out[0], gains, heads, own, *late)
    if rest:
        parts += pl.pallas_call(
            functools.partial(rest_kernel, rest),
            out_shape=[shape] * len(rest),
            in_specs=[vmem] * 4,
            out_specs=[vmem] * len(rest),
            compiler_params=pltpu.CompilerParams(vmem_limit_bytes=24 * 2**20),
            name="rest",
        )(mod, w_out[0], own, attended)
    parts = {order[i]: part for i, part in zip(first + rest, parts)}
    return reduce_scatter(parts, count)[None]


def solution(mesh):
    in_specs = (
        P("section", "seq", None),
        P("section", None, None),
        P("section", None, None, "seq"),
        P("section", None, None),
        P("section", "seq", None),
        P("section", None, None, "seq"),
        P("section"),
    )
    out_specs = P("section", "seq", None)
    return jax.shard_map(
        per_device, mesh=mesh, in_specs=in_specs, out_specs=out_specs, check_vma=False
    )
```

```python
import functools
import math

import jax
import jax.numpy as jnp
from jax import lax
from jax.experimental import pallas as pl
from jax.experimental.pallas import tpu as pltpu
from jax.sharding import PartitionSpec as P


def route(block, distance, sections_on=0):
    sections, count = lax.axis_size("section"), lax.axis_size("seq")
    pairs = [
        (s * count + i, (s + sections_on) % sections * count + (i ^ distance))
        for s in range(sections)
        for i in range(count)
    ]
    return lax.ppermute(block, ("section", "seq"), pairs)


def plan(count):
    if count == 8:
        return [(1, 0), (2, 0), (3, 0), (4, 0), (5, 4), (6, 4), (7, 4)]
    return [(r, r & (r - 1)) for r in range(1, count)]


def plan_back(count):
    if count == 8:
        return [(5, 4), (6, 4), (7, 4), (4, 0), (3, 0), (2, 0), (1, 0), (0, 0)]
    return [(r, r & (r - 1)) for r in reversed(range(count))]


def after(block, other):
    return lax.optimization_barrier((block, other))[0]


def gather(block, count, mixed):
    blocks = {0: block}
    for r, parent in plan(count):
        blocks[r] = route(blocks[parent], r ^ parent)
        if r == 4:
            blocks[r] = after(blocks[r], mixed)
    return blocks


def modulated(block, mod_ref):
    values = block.astype(jnp.float32)
    centred = values - jnp.mean(values, axis=-1, keepdims=True)
    spread = jnp.mean(centred * centred, axis=-1, keepdims=True)
    normed = centred * lax.rsqrt(spread + 1e-06)
    return (normed * (1.0 + mod_ref[1]) + mod_ref[0]).astype(jnp.bfloat16)


def early_kernel(mod_ref, *refs):
    blocks, mixed_ref = refs[:-1], refs[-1]
    rows = blocks[0].shape[0]
    for i, block in enumerate(blocks):
        mixed_ref[i * rows : (i + 1) * rows, :] = modulated(block[...], mod_ref)


def early_rows(mod, blocks):
    rows, width = blocks[0].shape
    vmem = pl.BlockSpec(memory_space=pltpu.VMEM)
    return pl.pallas_call(
        early_kernel,
        out_shape=jax.ShapeDtypeStruct((rows * len(blocks), width), jnp.bfloat16),
        in_specs=[vmem] * (1 + len(blocks)),
        out_specs=vmem,
        compiler_params=pltpu.CompilerParams(vmem_limit_bytes=12 * 2**20),
        cost_estimate=pl.CostEstimate(flops=2 * 10**9, bytes_accessed=64 * blocks[0].size, transcendentals=0),
        name="early",
    )(mod, *blocks)


def heads_of(mixed, gain_ref, qkv_ref):
    def part(j):
        return jnp.dot(mixed, qkv_ref[j], preferred_element_type=jnp.float32)

    def head_norm(values, gains):
        return values * lax.rsqrt(jnp.mean(values * values, axis=-1, keepdims=True) + 1e-06) * gains

    queries = head_norm(part(0), gain_ref[0:1, :]).astype(jnp.bfloat16)
    keys = head_norm(part(1), gain_ref[1:2, :]).astype(jnp.bfloat16)
    return queries, keys, part(2).astype(jnp.bfloat16)


def modulate_into(mixed, at, blocks, mod_ref):
    for block in blocks:
        mixed[at : at + block.shape[0], :] = modulated(block[...], mod_ref)
        at += block.shape[0]


def middle_kernel(mod_ref, gain_ref, qkv_ref, mixed_ref, *refs):
    blocks, heads_ref, mixed = refs[:-2], refs[-2], refs[-1]
    first = mixed_ref.shape[0]
    mixed[:first, :] = mixed_ref[...]
    modulate_into(mixed, first, blocks, mod_ref)
    for j, part in enumerate(heads_of(mixed[...], gain_ref, qkv_ref)):
        heads_ref[j] = part


def middle_heads(mod, gains, qkv, mixed, blocks):
    vmem = pl.BlockSpec(memory_space=pltpu.VMEM)
    tokens = mixed.shape[0] + sum(block.shape[0] for block in blocks)
    width, head = qkv.shape[1:]
    return pl.pallas_call(
        middle_kernel,
        out_shape=jax.ShapeDtypeStruct((3, tokens, head), jnp.bfloat16),
        in_specs=[vmem] * (4 + len(blocks)),
        out_specs=vmem,
        scratch_shapes=[pltpu.VMEM((tokens, width), jnp.bfloat16)],
        compiler_params=pltpu.CompilerParams(vmem_limit_bytes=24 * 2**20),
        cost_estimate=pl.CostEstimate(flops=10**9, bytes_accessed=2 * qkv.size, transcendentals=0),
        name="middle",
    )(mod, gains, qkv, mixed, *blocks)


def layer_kernel(count, outs_of, start_ref, mod_ref, qkv_ref, stale_ref, out_w_ref, gain_ref, heads_ref, own_ref, *refs):
    rows, width = own_ref.shape
    number = len(outs_of) + 1
    blocks, outs, attended_ref, mixed = refs[: -1 - number], refs[-1 - number : -2], refs[-2], refs[-1]
    head = qkv_ref.shape[2]
    clip = stale_ref.shape[1]
    patch = rows * count
    modulate_into(mixed, 0, blocks, mod_ref)
    queries, keys_new, values_new = [
        jnp.concatenate([heads_ref[j], part], axis=0)
        for j, part in enumerate(heads_of(mixed[...], gain_ref, qkv_ref))
    ]

    def scores_of(keys):
        raw = lax.dot_general(queries, keys, (((1,), (1,)), ((), ())), preferred_element_type=jnp.float32)
        return raw * (1.0 / math.sqrt(head))

    start = start_ref[0]
    clip_row = lax.broadcasted_iota(jnp.int32, (patch, clip), 1)
    replaced = (clip_row >= start) & (clip_row < start + patch)
    scores_new = scores_of(keys_new)
    scores_old = jnp.where(replaced, -jnp.inf, scores_of(stale_ref[0]))
    highest = jnp.maximum(
        jnp.max(scores_new, axis=-1, keepdims=True), jnp.max(scores_old, axis=-1, keepdims=True)
    )
    raised_new = jnp.exp(scores_new - highest)
    raised_old = jnp.exp(scores_old - highest)
    summed = jnp.sum(raised_new, axis=-1, keepdims=True) + jnp.sum(raised_old, axis=-1, keepdims=True)
    probs_new = (raised_new / summed).astype(jnp.bfloat16)
    probs_old = (raised_old / summed).astype(jnp.bfloat16)
    attended = jnp.dot(probs_new, values_new, preferred_element_type=jnp.float32) + jnp.dot(
        probs_old, stale_ref[1], preferred_element_type=jnp.float32
    )
    attended = attended.astype(jnp.bfloat16)
    attended_ref[...] = attended
    project_out(attended, outs_of, outs, mod_ref, out_w_ref, own_ref)


def project_out(attended, outs_of, outs, mod_ref, out_w_ref, own_ref):
    rows, width = own_ref.shape
    chosen = jnp.concatenate([attended[i * rows : (i + 1) * rows] for i in outs_of], axis=0)
    step = 512
    for at in range(0, width, step):
        columns = slice(at, at + step)
        part = jnp.dot(chosen, out_w_ref[:, columns], preferred_element_type=jnp.float32)
        part = part * mod_ref[2, :, columns]
        for k, out in enumerate(outs):
            piece = part[k * rows : (k + 1) * rows]
            if outs_of[k] == 0:
                piece = piece + own_ref[:, columns].astype(jnp.float32)
            out[:, columns] = piece.astype(jnp.bfloat16)


def rest_kernel(outs_of, mod_ref, out_w_ref, own_ref, attended_ref, *outs):
    project_out(attended_ref[...], outs_of, outs, mod_ref, out_w_ref, own_ref)


def add_up(*blocks):
    total = blocks[0].astype(jnp.float32)
    for block in blocks[1:]:
        total = total + block.astype(jnp.float32)
    return total.astype(jnp.bfloat16)


def reduce_scatter(parts, count):
    arrived = {r: [] for r in range(count)}
    for r, target in plan_back(count):
        total = add_up(parts[r], *arrived[r]) if r and arrived[r] else parts[r]
        arrived[target].append(route(total, r ^ target, int(target == 0)))
    return add_up(*arrived[0])


def per_device(hidden, modulation, w_qkv, qk_gain, w_out, stale_kv, patch_start):
    count = lax.axis_size("seq")
    tokens_in = hidden[0]
    rows, width = tokens_in.shape
    order = [0, 1, 2, 3, 4, 7, 6, 5] if count == 8 else list(range(count))
    mod, own = modulation.transpose(1, 0, 2), tokens_in
    mixed = early_rows(mod, [own])
    blocks = gather(tokens_in, count, mixed)
    vmem = pl.BlockSpec(memory_space=pltpu.VMEM)
    middle = count - 2
    qkv, gains = w_qkv[0].transpose(1, 0, 2), qk_gain[0]
    heads = middle_heads(mod, gains, qkv, mixed, [blocks[r] for r in order[1:middle]])
    late = [blocks[r] for r in order[middle:]]
    first = [order.index(r) for r in (count - 3, count - 2)]
    rest = [i for i in range(count) if i not in first]
    shape = jax.ShapeDtypeStruct((rows, width), jnp.bfloat16)
    head = qkv.shape[2]
    *parts, attended = pl.pallas_call(
        functools.partial(layer_kernel, count, first),
        out_shape=[shape] * len(first) + [jax.ShapeDtypeStruct((rows * count, head), jnp.bfloat16)],
        in_specs=[pl.BlockSpec(memory_space=pltpu.SMEM)] + [vmem] * (7 + len(late)),
        out_specs=[vmem] * (len(first) + 1),
        scratch_shapes=[pltpu.VMEM((rows * (count - middle), width), jnp.bfloat16)],
        compiler_params=pltpu.CompilerParams(vmem_limit_bytes=24 * 2**20),
        name="layer",
    )(patch_start, mod, qkv, stale_kv[0], w_out[0], gains, heads, own, *late)
    if rest:
        parts += pl.pallas_call(
            functools.partial(rest_kernel, rest),
            out_shape=[shape] * len(rest),
            in_specs=[vmem] * 4,
            out_specs=[vmem] * len(rest),
            compiler_params=pltpu.CompilerParams(vmem_limit_bytes=24 * 2**20),
            name="rest",
        )(mod, w_out[0], own, attended)
    parts = {order[i]: part for i, part in zip(first + rest, parts)}
    return reduce_scatter(parts, count)[None]


def solution(mesh):
    in_specs = (
        P("section", "seq", None),
        P("section", None, None),
        P("section", None, None, "seq"),
        P("section", None, None),
        P("section", "seq", None),
        P("section", None, None, "seq"),
        P("section"),
    )
    out_specs = P("section", "seq", None)
    return jax.shard_map(
        per_device, mesh=mesh, in_specs=in_specs, out_specs=out_specs, check_vma=False
    )
```

```python
import functools
import math

import jax
import jax.numpy as jnp
from jax import lax
from jax.experimental import pallas as pl
from jax.experimental.pallas import tpu as pltpu
from jax.sharding import PartitionSpec as P


def route(block, distance, sections_on=0):
    sections, count = lax.axis_size("section"), lax.axis_size("seq")
    pairs = [
        (s * count + i, (s + sections_on) % sections * count + (i ^ distance))
        for s in range(sections)
        for i in range(count)
    ]
    return lax.ppermute(block, ("section", "seq"), pairs)


def plan(count):
    if count == 8:
        return [(1, 0), (2, 0), (3, 0), (4, 0), (5, 4), (6, 4), (7, 4)]
    return [(r, r & (r - 1)) for r in range(1, count)]


def plan_back(count):
    if count == 8:
        return [(5, 4), (6, 4), (7, 4), (4, 0), (3, 0), (2, 0), (1, 0), (0, 0)]
    return [(r, r & (r - 1)) for r in reversed(range(count))]


def after(block, other):
    return lax.optimization_barrier((block, other))[0]


def gather(block, count, mixed):
    blocks = {0: block}
    for r, parent in plan(count):
        blocks[r] = route(blocks[parent], r ^ parent)
        if r == 4:
            blocks[r] = after(blocks[r], mixed)
    return blocks


def modulated(block, mod_ref):
    values = block.astype(jnp.float32)
    centred = values - jnp.mean(values, axis=-1, keepdims=True)
    spread = jnp.mean(centred * centred, axis=-1, keepdims=True)
    normed = centred * lax.rsqrt(spread + 1e-06)
    return (normed * (1.0 + mod_ref[1]) + mod_ref[0]).astype(jnp.bfloat16)


def early_kernel(mod_ref, *refs):
    blocks, mixed_ref = refs[:-1], refs[-1]
    rows = blocks[0].shape[0]
    for i, block in enumerate(blocks):
        mixed_ref[i * rows : (i + 1) * rows, :] = modulated(block[...], mod_ref)


def early_rows(mod, blocks):
    rows, width = blocks[0].shape
    vmem = pl.BlockSpec(memory_space=pltpu.VMEM)
    return pl.pallas_call(
        early_kernel,
        out_shape=jax.ShapeDtypeStruct((rows * len(blocks), width), jnp.bfloat16),
        in_specs=[vmem] * (1 + len(blocks)),
        out_specs=vmem,
        compiler_params=pltpu.CompilerParams(vmem_limit_bytes=12 * 2**20),
        cost_estimate=pl.CostEstimate(flops=2 * 10**9, bytes_accessed=64 * blocks[0].size, transcendentals=0),
        name="early",
    )(mod, *blocks)


def heads_of(mixed, gain_ref, qkv_ref):
    def part(j):
        return jnp.dot(mixed, qkv_ref[j], preferred_element_type=jnp.float32)

    def head_norm(values, gains):
        return values * lax.rsqrt(jnp.mean(values * values, axis=-1, keepdims=True) + 1e-06) * gains

    queries = head_norm(part(0), gain_ref[0:1, :]).astype(jnp.bfloat16)
    keys = head_norm(part(1), gain_ref[1:2, :]).astype(jnp.bfloat16)
    return queries, keys, part(2).astype(jnp.bfloat16)


def modulate_into(mixed, at, blocks, mod_ref):
    for block in blocks:
        mixed[at : at + block.shape[0], :] = modulated(block[...], mod_ref)
        at += block.shape[0]


def middle_kernel(mod_ref, gain_ref, qkv_ref, mixed_ref, *refs):
    blocks, heads_ref, mixed = refs[:-2], refs[-2], refs[-1]
    first = mixed_ref.shape[0]
    mixed[:first, :] = mixed_ref[...]
    modulate_into(mixed, first, blocks, mod_ref)
    for j, part in enumerate(heads_of(mixed[...], gain_ref, qkv_ref)):
        heads_ref[j] = part


def middle_heads(mod, gains, qkv, mixed, blocks):
    vmem = pl.BlockSpec(memory_space=pltpu.VMEM)
    tokens = mixed.shape[0] + sum(block.shape[0] for block in blocks)
    width, head = qkv.shape[1:]
    return pl.pallas_call(
        middle_kernel,
        out_shape=jax.ShapeDtypeStruct((3, tokens, head), jnp.bfloat16),
        in_specs=[vmem] * (4 + len(blocks)),
        out_specs=vmem,
        scratch_shapes=[pltpu.VMEM((tokens, width), jnp.bfloat16)],
        compiler_params=pltpu.CompilerParams(vmem_limit_bytes=24 * 2**20),
        cost_estimate=pl.CostEstimate(flops=10**9, bytes_accessed=2 * qkv.size, transcendentals=0),
        name="middle",
    )(mod, gains, qkv, mixed, *blocks)


def layer_kernel(count, outs_of, start_ref, mod_ref, qkv_ref, stale_ref, out_w_ref, gain_ref, heads_ref, own_ref, *refs):
    rows, width = own_ref.shape
    number = len(outs_of) + 1
    blocks, outs, attended_ref, mixed = refs[: -1 - number], refs[-1 - number : -2], refs[-2], refs[-1]
    head = qkv_ref.shape[2]
    clip = stale_ref.shape[1]
    patch = rows * count
    modulate_into(mixed, 0, blocks, mod_ref)
    queries, keys_new, values_new = [
        jnp.concatenate([heads_ref[j], part], axis=0)
        for j, part in enumerate(heads_of(mixed[...], gain_ref, qkv_ref))
    ]

    def scores_of(keys):
        raw = lax.dot_general(queries, keys, (((1,), (1,)), ((), ())), preferred_element_type=jnp.float32)
        return raw * (1.0 / math.sqrt(head))

    start = start_ref[0]
    clip_row = lax.broadcasted_iota(jnp.int32, (patch, clip), 1)
    replaced = (clip_row >= start) & (clip_row < start + patch)
    scores_new = scores_of(keys_new)
    scores_old = jnp.where(replaced, -jnp.inf, scores_of(stale_ref[0]))
    highest = jnp.maximum(
        jnp.max(scores_new, axis=-1, keepdims=True), jnp.max(scores_old, axis=-1, keepdims=True)
    )
    raised_new = jnp.exp(scores_new - highest)
    raised_old = jnp.exp(scores_old - highest)
    summed = jnp.sum(raised_new, axis=-1, keepdims=True) + jnp.sum(raised_old, axis=-1, keepdims=True)
    probs_new = (raised_new / summed).astype(jnp.bfloat16)
    probs_old = (raised_old / summed).astype(jnp.bfloat16)
    attended = jnp.dot(probs_new, values_new, preferred_element_type=jnp.float32) + jnp.dot(
        probs_old, stale_ref[1], preferred_element_type=jnp.float32
    )
    attended = attended.astype(jnp.bfloat16)
    attended_ref[...] = attended
    project_out(attended, outs_of, outs, mod_ref, out_w_ref, own_ref)


def project_out(attended, outs_of, outs, mod_ref, out_w_ref, own_ref):
    rows, width = own_ref.shape
    chosen = jnp.concatenate([attended[i * rows : (i + 1) * rows] for i in outs_of], axis=0)
    step = 512
    for at in range(0, width, step):
        columns = slice(at, at + step)
        part = jnp.dot(chosen, out_w_ref[:, columns], preferred_element_type=jnp.float32)
        part = part * mod_ref[2, :, columns]
        for k, out in enumerate(outs):
            piece = part[k * rows : (k + 1) * rows]
            if outs_of[k] == 0:
                piece = piece + own_ref[:, columns].astype(jnp.float32)
            out[:, columns] = piece.astype(jnp.bfloat16)


def rest_kernel(outs_of, mod_ref, out_w_ref, own_ref, attended_ref, *outs):
    project_out(attended_ref[...], outs_of, outs, mod_ref, out_w_ref, own_ref)


def add_up(*blocks):
    total = blocks[0].astype(jnp.float32)
    for block in blocks[1:]:
        total = total + block.astype(jnp.float32)
    return total.astype(jnp.bfloat16)


def reduce_scatter(parts, count):
    arrived = {r: [] for r in range(count)}
    for r, target in plan_back(count):
        total = add_up(parts[r], *arrived[r]) if r and arrived[r] else parts[r]
        arrived[target].append(route(total, r ^ target, int(target == 0)))
    return add_up(*arrived[0])


def per_device(hidden, modulation, w_qkv, qk_gain, w_out, stale_kv, patch_start):
    count = lax.axis_size("seq")
    tokens_in = hidden[0]
    rows, width = tokens_in.shape
    order = [0, 2, 1, 3, 4, 7, 6, 5] if count == 8 else list(range(count))
    mod, own = modulation.transpose(1, 0, 2), tokens_in
    mixed = early_rows(mod, [own])
    blocks = gather(tokens_in, count, mixed)
    vmem = pl.BlockSpec(memory_space=pltpu.VMEM)
    middle = count - 2
    qkv, gains = w_qkv[0].transpose(1, 0, 2), qk_gain[0]
    heads = middle_heads(mod, gains, qkv, mixed, [blocks[r] for r in order[1:middle]])
    late = [blocks[r] for r in order[middle:]]
    first = [order.index(r) for r in (count - 3, count - 2)]
    rest = [i for i in range(count) if i not in first]
    shape = jax.ShapeDtypeStruct((rows, width), jnp.bfloat16)
    head = qkv.shape[2]
    *parts, attended = pl.pallas_call(
        functools.partial(layer_kernel, count, first),
        out_shape=[shape] * len(first) + [jax.ShapeDtypeStruct((rows * count, head), jnp.bfloat16)],
        in_specs=[pl.BlockSpec(memory_space=pltpu.SMEM)] + [vmem] * (7 + len(late)),
        out_specs=[vmem] * (len(first) + 1),
        scratch_shapes=[pltpu.VMEM((rows * (count - middle), width), jnp.bfloat16)],
        compiler_params=pltpu.CompilerParams(vmem_limit_bytes=24 * 2**20),
        name="layer",
    )(patch_start, mod, qkv, stale_kv[0], w_out[0], gains, heads, own, *late)
    if rest:
        parts += pl.pallas_call(
            functools.partial(rest_kernel, rest),
            out_shape=[shape] * len(rest),
            in_specs=[vmem] * 4,
            out_specs=[vmem] * len(rest),
            compiler_params=pltpu.CompilerParams(vmem_limit_bytes=24 * 2**20),
            name="rest",
        )(mod, w_out[0], own, attended)
    parts = {order[i]: part for i, part in zip(first + rest, parts)}
    return reduce_scatter(parts, count)[None]


def solution(mesh):
    in_specs = (
        P("section", "seq", None),
        P("section", None, None),
        P("section", None, None, "seq"),
        P("section", None, None),
        P("section", "seq", None),
        P("section", None, None, "seq"),
        P("section"),
    )
    out_specs = P("section", "seq", None)
    return jax.shard_map(
        per_device, mesh=mesh, in_specs=in_specs, out_specs=out_specs, check_vma=False
    )
```
